128 devices in a mesh: head: 8 (over z, core), seq: 16 (over x, y).
Axes of the slice: x: 4, y: 4, z: 4, core: 2. Of those that a mesh axis runs over, the one named last changes fastest.
Arguments:
- queries: bfloat16 [16384, 16, 128], P('seq', 'head'), may hold values from -14 to 14
- keys: bfloat16 [16384, 16, 128], P('seq', 'head'), may hold values from -14 to 14
- values: bfloat16 [16384, 16, 128], P('seq', 'head'), may hold values from -6 to 6
- out_grad: bfloat16 [16384, 16, 128], P('seq', 'head'), may hold values from -6 to 6
- cluster_ids: int32 [16, 16384, 1], P('head', 'seq'), may hold values from 0 to 191; in each aligned block of 1024 rows (0 to 1023, 1024 to 2047, ..., all dimensions but the last counted through in order) at most 8 rows name the same one
- query_weight: bfloat16 [2048, 16, 128], P(None, 'head'), may hold values from -0.125 to 0.125
- key_weight: bfloat16 [2048, 16, 128], P(None, 'head'), may hold values from -0.125 to 0.125
- value_weight: bfloat16 [2048, 16, 128], P(None, 'head'), may hold values from -0.125 to 0.125
Outputs:
- query_gradient: bfloat16 [16384, 16, 128], P('seq', 'head')
- key_gradient: bfloat16 [16384, 16, 128], P('seq', 'head')
- value_gradient: bfloat16 [16384, 16, 128], P('seq', 'head')
- input_grad: bfloat16 [2048, 16384], P('head', 'seq')
- key_sums: float32 [16, 192, 128], P('head', 'seq')
The draws below stay inside these ranges and needn't reach their ends.
Inputs may be any that keep to these rules, and one draw needn't show every extreme that they name: `cluster_ids`: in each head, no cluster holds more than 8 of the tokens of one index of seq.
All inputs are finite; a program needn't handle non-finite values.
Results may differ from the reference program's by a relative error of at most 0.028.
The reference program's roundings to bfloat16 on the way count: a program that leaves them out, or rounds other values in their place, can miss the bound.
Values may be sent and summed in bfloat16 or wider, within the bound.
No kernel may reach another device: no remote copies, remote signals or barrier semaphores. Data moves between devices by JAX's collectives and lax.ppermute only.
A program may use at most 64 MiB of HBM per device.

```python
import math
import jax
import jax.numpy as jnp
import numpy as np
from jax import lax

HEAD_DIM = 128
HEAD_DEV = 2
MODEL = 2048
CLUSTERS = 192
TOK_DEV = 1024
SLOTS = 8
HEADS = 16
TOKENS = 16384
N_SEQ = 16


def drawn_rows(key, salt):
    noise = jax.random.normal(jax.random.fold_in(key, salt), (TOKENS, HEADS, HEAD_DIM), jnp.float32)
    return jnp.clip(noise, -6.0, 6.0).astype(jnp.bfloat16)


def draw_queries(key, part):
    return drawn_rows(key, 21)


def draw_keys(key, part):
    return drawn_rows(key, 41)


def shard_levels(key, extent, split, least, top_value):
    factor_of, own = 1.0, jax.random.fold_in(key, 6)
    for axis_at, shards_of in split:
        draws = jnp.exp(jax.random.uniform(jax.random.fold_in(own, axis_at), (shards_of,), jnp.float32, least / len(split), top_value / len(split)))
        factor_of = factor_of * jnp.repeat(draws, extent[axis_at] // shards_of).reshape([-1 if axis == axis_at else 1 for axis in range(len(extent))])
    return factor_of


def assign_block(key, own, number, rows, number_of, top, reach, skew):
    sequence = jax.random.permutation(key, number_of)
    packed, usual = shares(number_of, rows * top, reach, skew, True), shares(number_of, rows * top, reach, skew, False)
    places = jnp.arange(number_of)

    def named(lengths, turn):
        used = int((lengths > 0).sum())
        fixed = max(1, used // 4)
        shifted = fixed + (places - fixed + turn * (used - fixed)) % max(1, number_of - fixed)
        return jnp.zeros((number_of,), jnp.int32).at[sequence[jnp.where(places < fixed, places, shifted)]].set(jnp.asarray(lengths, jnp.int32))

    lengths = jnp.where(number % 4 == 0, named(packed, number // 4), named(usual, number - number // 4 - 1))
    mixed = jax.random.permutation(jax.random.fold_in(own, 3), number_of)
    giver, taker = mixed[0:number_of // 2 * 2:2], mixed[1:number_of // 2 * 2:2]
    margin = jnp.minimum(lengths[giver] - 1, reach - lengths[taker]) // 2
    margin = jnp.where((giver == sequence[0]) | (taker == sequence[0]) | (lengths[taker] == 0), 0, jnp.maximum(margin, 0))
    shifted = jax.random.randint(jax.random.fold_in(own, 4), (number_of // 2,), 0, 1 << 20) % (margin + 1)
    lengths = lengths.at[giver].add(-shifted).at[taker].add(shifted)
    labels = jnp.searchsorted(jnp.cumsum(lengths), jnp.arange(rows * top), side="right").astype(jnp.int32)
    grid = labels.reshape(top, rows).T
    grid = grid[jax.random.permutation(jax.random.fold_in(own, 1), rows)]
    turn = jax.random.randint(jax.random.fold_in(own, 2), (rows, 1), 0, top)
    return jnp.take_along_axis(grid, (jnp.arange(top)[None, :] + turn) % top, axis=1)


def shares(number_of, total, most, lean, full):
    loads = [(1 << 20) // math.isqrt(grade ** lean) + 1 for grade in range(1, number_of + 1)]
    largest = most if full else min(most, max(-(-total // number_of), total * loads[0] // sum(loads)))
    least = 1 if total - largest >= number_of - 1 else 0
    given, spare = [largest] + [least] * (number_of - 1), total - largest - least * (number_of - 1)
    while spare > 0:
        candidates = [i for i in range(1, number_of) if given[i] < largest] or [i for i in range(1, number_of) if given[i] < most]
        pool, budget = sum([loads[i] for i in candidates]), spare
        for i in candidates:
            more = min(most - given[i], max(1, budget * loads[i] // pool), spare)
            given[i] = given[i] + more
            spare = spare - more
    return np.array(given)


def gaussian(key, shape, spread, bound, pieces=(), kind=jnp.bfloat16):
    values = spread * jax.random.normal(key, shape, jnp.float32)
    if pieces:
        values = values * shard_levels(key, shape, pieces, -0.22, 0.18)
    return jnp.clip(values, -bound, bound).astype(kind)


def setup_inputs(seed: int = 0) -> dict:
    splits = jax.random.split(jax.random.key(seed), 9)
    queries = draw_queries(jax.random.fold_in(splits[8], 71), 0)
    keys = draw_keys(jax.random.fold_in(splits[8], 71), 0)
    values = gaussian(splits[2], (TOKENS, HEADS, HEAD_DIM), 1.0, 6.0, ((0, 16), (1, 8)))
    out_grad = gaussian(splits[3], (TOKENS, HEADS, HEAD_DIM), 1.0, 6.0, ((0, 16), (1, 8)))
    cluster_ids_keys = jax.random.split(jax.random.fold_in(splits[4], 1), HEADS * TOKENS // TOK_DEV)
    cluster_ids_turns = jax.random.permutation(jax.random.fold_in(splits[4], 3), HEADS * TOKENS // TOK_DEV)
    cluster_ids = jax.vmap(lambda own, number: assign_block(jax.random.fold_in(splits[4], 2), own, number, TOK_DEV, CLUSTERS, 1, SLOTS, 2))(cluster_ids_keys, cluster_ids_turns).reshape((HEADS, TOKENS, 1))
    query_weight = gaussian(splits[5], (MODEL, HEADS, HEAD_DIM), MODEL ** -0.5, 0.125, ((1, 8),))
    key_weight = gaussian(splits[6], (MODEL, HEADS, HEAD_DIM), MODEL ** -0.5, 0.125, ((1, 8),))
    value_weight = gaussian(splits[7], (MODEL, HEADS, HEAD_DIM), MODEL ** -0.5, 0.125, ((1, 8),))
    return {"queries": queries, "keys": keys, "values": values, "out_grad": out_grad, "cluster_ids": cluster_ids, "query_weight": query_weight, "key_weight": key_weight, "value_weight": value_weight}


def cluster_grads(qb, kb, vb, gb, live):
    scale = 1.0 / math.sqrt(HEAD_DIM)
    count = qb.shape[0]
    position = jnp.arange(count, dtype=jnp.int32)
    allowed = (position[None, :] <= position[:, None]) & live[None, :] | (position[None, :] == position[:, None])
    scores = jnp.dot(qb, kb.T, preferred_element_type=jnp.float32) * scale
    scores = jnp.where(allowed, scores, jnp.float32(-1e+30))
    top = lax.optimization_barrier(jnp.max(scores, axis=-1, keepdims=True))
    expo = jnp.where(allowed, jnp.exp(scores - top), jnp.float32(0.0))
    probs = expo / lax.optimization_barrier(jnp.sum(expo, axis=-1, keepdims=True))
    probs_b = probs.astype(jnp.bfloat16)
    attended = jnp.dot(probs_b, vb, preferred_element_type=jnp.float32)
    delta = lax.optimization_barrier(jnp.sum(gb.astype(jnp.float32) * attended, axis=-1))
    dprob = jnp.dot(gb, vb.T, preferred_element_type=jnp.float32)
    dscore = (probs * (dprob - delta[:, None]) * scale).astype(jnp.bfloat16)
    grad_q = jnp.dot(dscore, kb, preferred_element_type=jnp.float32).astype(jnp.bfloat16)
    grad_k = jnp.dot(dscore.T, qb, preferred_element_type=jnp.float32).astype(jnp.bfloat16)
    grad_v = jnp.dot(probs_b.T, gb, preferred_element_type=jnp.float32).astype(jnp.bfloat16)
    return (grad_q, grad_k, grad_v)

def head_grads(q_head, k_head, v_head, g_head, ids_head):
    capacity = SLOTS * N_SEQ
    tokens_all = ids_head.shape[0]
    order = jnp.argsort(ids_head, stable=True).astype(jnp.int32)
    sorted_ids = ids_head[order]
    counts = jax.ops.segment_sum(jnp.ones((tokens_all,), jnp.int32), ids_head, CLUSTERS)
    starts = (jnp.cumsum(counts) - counts).astype(jnp.int32)
    sorted_flat = sorted_ids * capacity + jnp.arange(tokens_all, dtype=jnp.int32) - starts[sorted_ids]
    flat = jnp.zeros((tokens_all,), jnp.int32).at[order].set(sorted_flat.astype(jnp.int32))

    def pack(x):
        return jnp.zeros((CLUSTERS * capacity, HEAD_DIM), x.dtype).at[flat].set(x).reshape(CLUSTERS, capacity, HEAD_DIM)
    live = jnp.zeros((CLUSTERS * capacity,), bool).at[flat].set(True).reshape(CLUSTERS, capacity)
    grad_q, grad_k, grad_v = jax.vmap(cluster_grads)(pack(q_head), pack(k_head), pack(v_head), pack(g_head), live)

    def unpack(buffer):
        return buffer.reshape(CLUSTERS * capacity, HEAD_DIM)[flat]
    sums = jax.ops.segment_sum(k_head.astype(jnp.float32), ids_head, CLUSTERS) / math.sqrt(capacity)
    return (unpack(grad_q), unpack(grad_k), unpack(grad_v), sums)

def reference(queries, keys, values, out_grad, cluster_ids, query_weight, key_weight, value_weight):
    grads_q, grads_k, grads_v, sums_all = ([], [], [], [])
    for head in range(HEADS):
        grad_q, grad_k, grad_v, sums = head_grads(queries[:, head], keys[:, head], values[:, head], out_grad[:, head], cluster_ids[head, :, 0])
        grads_q.append(grad_q)
        grads_k.append(grad_k)
        grads_v.append(grad_v)
        sums_all.append(sums)
    query_gradient = jnp.stack(grads_q, axis=1)
    key_gradient = jnp.stack(grads_k, axis=1)
    value_gradient = jnp.stack(grads_v, axis=1)
    key_sums = jnp.stack(sums_all, axis=0)
    grand_total = jnp.zeros((MODEL, query_gradient.shape[0]), jnp.float32)
    for group in range(HEADS // HEAD_DEV):
        term = jnp.zeros((MODEL, query_gradient.shape[0]), jnp.float32)
        for head in range(group * HEAD_DEV, (group + 1) * HEAD_DEV):
            term = term + jnp.dot(query_weight[:, head], query_gradient[:, head].T, preferred_element_type=jnp.float32)
            term = term + jnp.dot(key_weight[:, head], key_gradient[:, head].T, preferred_element_type=jnp.float32)
            term = term + jnp.dot(value_weight[:, head], value_gradient[:, head].T, preferred_element_type=jnp.float32)
        grand_total = grand_total + lax.optimization_barrier(term.astype(jnp.bfloat16)).astype(jnp.float32)
    input_grad = grand_total.astype(jnp.bfloat16)
    return (query_gradient, key_gradient, value_gradient, input_grad, key_sums)
```

```python
import math

import jax
import jax.numpy as jnp
from jax import lax
from jax.experimental import pallas as pl
from jax.experimental.pallas import tpu as pltpu
from jax.sharding import PartitionSpec as P

CLUSTERS = 192
SLOTS = 8
WIDTH = 128
TOK = 1024
SEQ = 16
CL_DEV = CLUSTERS // SEQ
ROWS = CLUSTERS * SLOTS
EMPTY = 1024.0
LIMIT = 100.0
VMEM = 56 * 1024 * 1024

f32 = jnp.float32
bf16 = jnp.bfloat16


def dot(a, b):
    return jnp.dot(a, b, preferred_element_type=f32)


def dot_nt(a, b):
    return lax.dot_general(a, b, (((1,), (1,)), ((), ())), preferred_element_type=f32)


def dot_tn(a, b):
    return lax.dot_general(a, b, (((0,), (0,)), ((), ())), preferred_element_type=f32)


def iota(shape, axis):
    return lax.broadcasted_iota(jnp.int32, shape, axis)


def pack_kernel(ids_ref, q_ref, k_ref, v_ref, g_ref, out_ref, flat_ref, rows_ref):
    i, j = iota((256, 256), 0), iota((256, 256), 1)
    split = (j == jnp.where(i < 128, 2 * i, 2 * i - 255)).astype(f32).astype(bf16)
    for b in range(TOK // 128):
        block = jnp.concatenate(
            [ref[256 * b : 256 * (b + 1), :] for ref in (q_ref, k_ref, v_ref, g_ref)], axis=1
        )
        parted = dot(split, block).astype(bf16)
        rows_ref[0, 128 * b : 128 * (b + 1), :] = parted[:128]
        rows_ref[1, 128 * b : 128 * (b + 1), :] = parted[128:]
    u, t = iota((256, 512), 0), iota((256, 512), 1)
    earlier = ((u < t) | (t >= 256)).astype(f32).astype(bf16)
    flats = []
    for h in range(2):
        ids = ids_ref[h]
        member = iota((CLUSTERS, TOK), 0) == ids
        member_b = member.astype(f32).astype(bf16)
        carry = jnp.zeros((CLUSTERS, 256), f32)
        ranks = []
        for b in range(TOK // 256):
            sums = dot(member_b[:, 256 * b : 256 * (b + 1)], earlier)
            before = sums[:, :256] + carry
            carry = carry + sums[:, 256:]
            mine = jnp.where(member[:, 256 * b : 256 * (b + 1)], before, 0.0)
            ranks.append(jnp.sum(mine, axis=0, keepdims=True))
        flat = ids * SLOTS + jnp.concatenate(ranks, axis=1).astype(jnp.int32)
        flat_ref[h] = flat
        flats.append(flat)
    dsts = 2
    step = dsts * CL_DEV * SLOTS
    slot = iota((step, TOK), 0)
    for j in range(SEQ // dsts):
        parts = []
        for h in range(2):
            place = (slot == flats[h] - j * step).astype(f32)
            used = jnp.sum(place, axis=1, keepdims=True) > 0.0
            moved = dot(place.astype(bf16), rows_ref[h])
            parts.append((moved, used))
        for x in range(4):
            halves = []
            for moved, used in parts:
                piece = moved[:, WIDTH * x : WIDTH * (x + 1)]
                if x == 1:
                    piece = jnp.where(used, piece, EMPTY)
                halves.append(piece.reshape(dsts * CL_DEV, SLOTS, WIDTH))
            tile = jnp.concatenate(halves, axis=1).astype(bf16)
            out_ref[dsts * j : dsts * (j + 1), x] = tile.reshape(dsts, CL_DEV, 2 * SLOTS, WIDTH)


def pack(ids, q, k, v, g):
    return pl.pallas_call(
        pack_kernel,
        out_shape=(
            jax.ShapeDtypeStruct((SEQ, 4, CL_DEV, 2 * SLOTS, WIDTH), bf16),
            jax.ShapeDtypeStruct((2, 1, TOK), jnp.int32),
        ),
        scratch_shapes=[pltpu.VMEM((2, TOK, 4 * WIDTH), bf16)],
        compiler_params=pltpu.CompilerParams(vmem_limit_bytes=VMEM),
        name="pack",
    )(ids, q, k, v, g)


PER_STEP = 4


def attend_kernel(in_ref, out_ref, sums_ref):
    scale = 1.0 / math.sqrt(WIDTH)
    count = SEQ * SLOTS
    key, query = iota((count, count), 0), iota((count, count), 1)
    causal, diagonal = key < query, key == query
    items = []
    for c in range(PER_STEP):
        wide = [in_ref[:, x, c].astype(f32) for x in range(4)]
        for h in range(2):
            items.append(
                [w[:, SLOTS * h : SLOTS * (h + 1)].reshape(count, WIDTH) for w in wide]
            )
    sums, grads = [], []
    for q32, k32, v32, g32 in items:
        q, k, v, g = (x.astype(bf16) for x in (q32, k32, v32, g32))
        empty = k32 > LIMIT
        sums.append(jnp.sum(jnp.where(empty, 0.0, k32), axis=0, keepdims=True))
        allowed = (causal & jnp.logical_not(empty)) | diagonal
        score = jnp.where(allowed, dot_nt(k, q) * scale, -1e30)
        dprob = dot_nt(v, g)
        top = jnp.max(score, axis=0, keepdims=True)
        expo = jnp.exp(score - top)
        prob = expo / jnp.sum(expo, axis=0, keepdims=True)
        prob_b = prob.astype(bf16)
        delta = jnp.sum(prob_b.astype(f32) * dprob, axis=0, keepdims=True)
        dscore = (prob * (dprob - delta) * scale).astype(bf16)
        grads.append((dot_tn(dscore, k), dot(dscore, q), dot(prob_b, g)))
    for c in range(PER_STEP):
        for x in range(3):
            halves = [grads[2 * c + h][x].reshape(SEQ, SLOTS, WIDTH) for h in range(2)]
            out_ref[:, x, c] = jnp.concatenate(halves, axis=1).astype(bf16)
    sums_ref[0] = jnp.concatenate(sums, axis=0) * scale


def attend(got):
    steps = CL_DEV // PER_STEP
    return pl.pallas_call(
        attend_kernel,
        grid=(steps,),
        in_specs=[
            pl.BlockSpec((SEQ, 4, PER_STEP, 2 * SLOTS, WIDTH), lambda i: (0, 0, i, 0, 0)),
        ],
        out_specs=(
            pl.BlockSpec((SEQ, 3, PER_STEP, 2 * SLOTS, WIDTH), lambda i: (0, 0, i, 0, 0)),
            pl.BlockSpec((1, 2 * PER_STEP, WIDTH), lambda i: (i, 0, 0)),
        ),
        out_shape=(
            jax.ShapeDtypeStruct((SEQ, 3, CL_DEV, 2 * SLOTS, WIDTH), bf16),
            jax.ShapeDtypeStruct((steps, 2 * PER_STEP, WIDTH), f32),
        ),
        compiler_params=pltpu.CompilerParams(vmem_limit_bytes=VMEM),
        name="attend",
    )(got)


def unpack_kernel(flat_ref, in_ref, q_ref, k_ref, v_ref, all_ref, rows_ref):
    for x in range(3):
        wide = in_ref[:, x].astype(f32)
        for h in range(2):
            part = wide[:, :, SLOTS * h : SLOTS * (h + 1)].reshape(ROWS, WIDTH)
            rows_ref[h, :, WIDTH * x : WIDTH * (x + 1)] = part.astype(bf16)
    columns = []
    for h in range(2):
        line = jnp.broadcast_to(flat_ref[h].astype(f32), (8, TOK))
        columns.append(line.T[:, :1].astype(jnp.int32))
    i, j = iota((256, 256), 0), iota((256, 256), 1)
    merge = (i == jnp.where(j < 128, 2 * j, 2 * j - 255)).astype(f32).astype(bf16)
    slot = iota((256, ROWS), 1)
    for b in range(TOK // 256):
        found = []
        for h in range(2):
            place = (slot == columns[h][256 * b : 256 * (b + 1)]).astype(f32).astype(bf16)
            rows = dot(place, rows_ref[h]).astype(bf16)
            all_ref[256 * b : 256 * (b + 1), 384 * h : 384 * (h + 1)] = rows
            found.append(rows)
        for s in range(2):
            both = jnp.concatenate([rows[128 * s : 128 * (s + 1)] for rows in found], axis=0)
            mixed = dot(merge, both).astype(bf16)
            at = 512 * b + 256 * s
            q_ref[at : at + 256, :] = mixed[:, :128]
            k_ref[at : at + 256, :] = mixed[:, 128:256]
            v_ref[at : at + 256, :] = mixed[:, 256:]


def unpack(flat, got):
    one = jax.ShapeDtypeStruct((2 * TOK, WIDTH), bf16)
    return pl.pallas_call(
        unpack_kernel,
        out_shape=(one, one, one, jax.ShapeDtypeStruct((TOK, 6 * WIDTH), bf16)),
        scratch_shapes=[pltpu.VMEM((2, ROWS, 3 * WIDTH), bf16)],
        compiler_params=pltpu.CompilerParams(vmem_limit_bytes=VMEM),
        name="unpack",
    )(flat, got)


def shards(queries, keys, values, out_grad, cluster_ids, query_weight, key_weight, value_weight):
    place = lax.axis_index("head")
    core, z = place % 2, place // 2
    swap = [(i, i ^ 1) for i in range(8)]
    up = [(i, (i + 2) % 8) for i in range(8)]
    down = [(i, (i - 2) % 8) for i in range(8)]

    def blocks(which):
        parts = [w.reshape(4, 2, 256, 2, WIDTH) for w in (query_weight, key_weight, value_weight)]
        parts = [lax.dynamic_index_in_dim(w, which, 1, keepdims=False) for w in parts]
        whole = jnp.stack(parts, axis=3).reshape(4, 256, 6 * WIDTH)
        return jnp.roll(whole, -z, axis=0)

    weight_own = blocks(core)
    weight_other = lax.ppermute(blocks(1 - core), "head", swap)

    ids = jnp.transpose(cluster_ids, (0, 2, 1))
    flat2 = [x.reshape(2 * TOK, WIDTH) for x in (queries, keys, values, out_grad)]
    sent, flat = pack(ids, *flat2)
    got = lax.all_to_all(sent, "seq", split_axis=0, concat_axis=0, tiled=True)
    back, sums = attend(got)
    key_sums = jnp.transpose(sums.reshape(CL_DEV, 2, WIDTH), (1, 0, 2))
    home = lax.all_to_all(back, "seq", split_axis=0, concat_axis=0, tiled=True)
    grad_q, grad_k, grad_v, own = unpack(flat, home)
    other = lax.ppermute(own, "head", swap)

    def part(j, lo=0, hi=256):
        return dot_nt(weight_own[j, lo:hi], own) + dot_nt(weight_other[j, lo:hi], other)

    far = part(2).astype(bf16)
    up_far = lax.ppermute(far[:128], "head", up)
    down_far = lax.ppermute(far[128:], "head", down)
    up_near = lax.ppermute(part(1, 128, 256).astype(bf16), "head", up)
    down_near = lax.ppermute(part(3, 0, 128).astype(bf16), "head", down)
    up_sum = lax.ppermute((part(1, 0, 128) + up_far.astype(f32)).astype(bf16), "head", up)
    down_sum = lax.ppermute((part(3, 128, 256) + down_far.astype(f32)).astype(bf16), "head", down)
    mine = part(0)
    first = mine[:128] + up_sum.astype(f32) + down_near.astype(f32)
    last = mine[128:] + up_near.astype(f32) + down_sum.astype(f32)
    input_grad = jnp.concatenate([first, last], axis=0).astype(bf16)
    grads = [x.reshape(TOK, 2, WIDTH) for x in (grad_q, grad_k, grad_v)]
    return (*grads, input_grad, key_sums)


def solution(mesh):
    placed = (
        P("seq", "head", None),
        P("seq", "head", None),
        P("seq", "head", None),
        P("seq", "head", None),
        P("head", "seq", None),
        P(None, "head", None),
        P(None, "head", None),
        P(None, "head", None),
    )
    return jax.shard_map(
        shards,
        mesh=mesh,
        in_specs=placed,
        out_specs=(
            P("seq", "head", None),
            P("seq", "head", None),
            P("seq", "head", None),
            P("head", "seq"),
            P("head", "seq", None),
        ),
        check_vma=False,
    )
```

```python
import functools
import math

import jax
import jax.numpy as jnp
from jax import lax
from jax.experimental import pallas as pl
from jax.experimental.pallas import tpu as pltpu
from jax.sharding import PartitionSpec as P

CLUSTERS = 192
SLOTS = 8
WIDTH = 128
TOK = 1024
HALF = TOK // 2
SEQ = 16
CL_DEV = CLUSTERS // SEQ
RUN = CL_DEV * SLOTS
ROWS = CLUSTERS * SLOTS
QUARTER = 256
EMPTY = 1024.0
LIMIT = 100.0
PACK_DSTS = 2

f32 = jnp.float32
bf16 = jnp.bfloat16
WHOLE = pl.BlockSpec(memory_space=pltpu.VMEM)
MIB = 1024 * 1024


def near(x):
    return pltpu.with_memory_space_constraint(x, pltpu.VMEM)


def dot(a, b):
    return jnp.dot(a, b, preferred_element_type=f32)


def dot_nt(a, b):
    return lax.dot_general(a, b, (((1,), (1,)), ((), ())), preferred_element_type=f32)


def dot_tn(a, b):
    return lax.dot_general(a, b, (((0,), (0,)), ((), ())), preferred_element_type=f32)


def iota(shape, axis):
    return lax.broadcasted_iota(jnp.int32, shape, axis)


def pack_kernel(ids_ref, q_ref, k_ref, v_ref, g_ref, out_ref, flat_ref, pairs_ref, rows_ref, sem):
    copies = []
    for x, ref in enumerate((q_ref, k_ref, v_ref, g_ref)):
        copy = pltpu.make_async_copy(ref, pairs_ref.at[x], sem.at[x])
        copy.start()
        copies.append(copy)
    u, t = iota((256, 512), 0), iota((256, 512), 1)
    earlier = ((u < t) | (t >= 256)).astype(f32).astype(bf16)
    ids = [ids_ref[h] for h in range(2)]
    cluster = iota((CLUSTERS, 256), 0)
    carry = jnp.zeros((2 * CLUSTERS, 256), f32)
    ranks = [[], []]
    for b in range(TOK // 256):
        member = jnp.concatenate(
            [(cluster == line[:, 256 * b : 256 * (b + 1)]).astype(f32) for line in ids], axis=0
        )
        sums = dot(member.astype(bf16), earlier)
        mine = member * (sums[:, :256] + carry)
        carry = carry + sums[:, 256:]
        for h in range(2):
            part = mine[CLUSTERS * h : CLUSTERS * (h + 1)]
            ranks[h].append(jnp.sum(part, axis=0, keepdims=True))
    flats = []
    for h in range(2):
        flat = ids[h] * SLOTS + jnp.concatenate(ranks[h], axis=1).astype(jnp.int32)
        flat_ref[h] = flat
        flats.append(flat)
    for copy in copies:
        copy.wait()
    i, j = iota((256, 256), 0), iota((256, 256), 1)
    split = (j == jnp.where(i < 128, 2 * i, 2 * i - 255)).astype(f32).astype(bf16)
    for b in range(TOK // 128):
        block = jnp.concatenate([pairs_ref[x, 256 * b : 256 * (b + 1), :] for x in range(4)], axis=1)
        parted = dot(split, block).astype(bf16)
        rows_ref[0, 128 * b : 128 * (b + 1), :] = parted[:128]
        rows_ref[1, 128 * b : 128 * (b + 1), :] = parted[128:]
    step = PACK_DSTS * RUN
    slot = iota((step, TOK), 0)
    groups = (PACK_DSTS * CL_DEV, SLOTS, WIDTH)
    rank = iota(groups, 1).astype(f32)
    for j in range(SEQ // PACK_DSTS):
        for h in range(2):
            place = (slot == flats[h] - j * step).astype(f32).astype(bf16)
            moved = dot(place, rows_ref[h])
            for x in range(4):
                piece = moved[:, WIDTH * x : WIDTH * (x + 1)]
                if x == 1:
                    at = CLUSTERS * h + groups[0] * j
                    count = jnp.broadcast_to(carry[at : at + groups[0], None, :WIDTH], groups)
                    piece = jnp.where(rank < count, piece.reshape(groups), EMPTY)
                piece = piece.reshape(PACK_DSTS, RUN, WIDTH).astype(bf16)
                out_ref[PACK_DSTS * j : PACK_DSTS * (j + 1), x, h] = piece


def pack(ids, *tensors):
    far = [pltpu.with_memory_space_constraint(x, pltpu.HBM) for x in tensors]
    return pl.pallas_call(
        pack_kernel,
        in_specs=[WHOLE] + [pl.BlockSpec(memory_space=pltpu.HBM)] * 4,
        out_specs=(WHOLE, WHOLE),
        out_shape=(
            pltpu.VMEM((SEQ, 4, 2, RUN, WIDTH), bf16),
            jax.ShapeDtypeStruct((2, 1, TOK), jnp.int32),
        ),
        scratch_shapes=[
            pltpu.VMEM((4, 2 * TOK, WIDTH), bf16),
            pltpu.VMEM((2, TOK, 4 * WIDTH), bf16),
            pltpu.SemaphoreType.DMA((4,)),
        ],
        compiler_params=pltpu.CompilerParams(vmem_limit_bytes=16 * MIB),
        name="pack",
    )(ids, *far)


def attend_kernel(in_ref, back_ref, sums_ref, qkg_ref, pd_ref, out_ref, sem):
    scale = 1.0 / math.sqrt(WIDTH)
    count = SEQ * SLOTS
    key, query = iota((count, count), 0), iota((count, count), 1)
    causal, diagonal = key < query, key == query
    spots = [(h, c) for h in range(2) for c in range(0, CL_DEV, 2)]
    for h, c in spots:
        wide = [in_ref[:, x, h, SLOTS * c : SLOTS * (c + 2)].astype(f32) for x in range(4)]
        for s in range(2):
            q32, k32, v32, g32 = [
                w[:, SLOTS * s : SLOTS * (s + 1)].reshape(count, WIDTH) for w in wide
            ]
            q, k, v, g = (x.astype(bf16) for x in (q32, k32, v32, g32))
            for x, y in enumerate((q, k, g)):
                qkg_ref[h, c + s, x] = y
            empty = k32 > LIMIT
            total = jnp.sum(jnp.where(empty, 0.0, k32), axis=0, keepdims=True)
            sums_ref[c + s, h : h + 1] = total * scale
            allowed = (causal & jnp.logical_not(empty)) | diagonal
            score = jnp.where(allowed, dot_nt(k, q) * scale, -1e30)
            dprob = dot_nt(v, g)
            top = jnp.max(score, axis=0, keepdims=True)
            expo = jnp.exp(score - top)
            prob = expo * (1.0 / jnp.sum(expo, axis=0, keepdims=True))
            prob_b = prob.astype(bf16)
            delta = jnp.sum(prob_b.astype(f32) * dprob, axis=0, keepdims=True)
            pd_ref[h, c + s, 0] = prob_b
            pd_ref[h, c + s, 1] = (prob * (dprob - delta) * scale).astype(bf16)
    copies = []
    for h in range(2):
        for x in range(3):
            for c in range(0, CL_DEV, 2):
                halves = []
                for s in range(2):
                    first, second = pd_ref[h, c + s, 0 if x == 2 else 1], qkg_ref[h, c + s, (1, 0, 2)[x]]
                    grad = dot_tn(first, second) if x == 0 else dot(first, second)
                    halves.append(grad.reshape(SEQ, SLOTS, WIDTH))
                tile = jnp.concatenate(halves, axis=1).astype(bf16)
                out_ref[:, x, h, SLOTS * c : SLOTS * (c + 2)] = tile
            copy = pltpu.make_async_copy(out_ref.at[:, x, h], back_ref.at[:, x, h], sem.at[h, x])
            copy.start()
            copies.append(copy)
    for copy in copies:
        copy.wait()


def attend(got):
    return pl.pallas_call(
        attend_kernel,
        in_specs=[WHOLE],
        out_specs=(pl.BlockSpec(memory_space=pltpu.HBM), WHOLE),
        out_shape=(
            pltpu.HBM((SEQ, 3, 2, RUN, WIDTH), bf16),
            jax.ShapeDtypeStruct((CL_DEV, 2, WIDTH), f32),
        ),
        scratch_shapes=[
            pltpu.VMEM((2, CL_DEV, 3, SEQ * SLOTS, WIDTH), bf16),
            pltpu.VMEM((2, CL_DEV, 2, SEQ * SLOTS, SEQ * SLOTS), bf16),
            pltpu.VMEM((SEQ, 3, 2, RUN, WIDTH), bf16),
            pltpu.SemaphoreType.DMA((2, 3)),
        ],
        compiler_params=pltpu.CompilerParams(vmem_limit_bytes=12 * MIB),
        name="attend",
    )(near(got))


def unpack_kernel(half, flat_ref, in_ref, own_ref):
    slot = iota((HALF, ROWS), 1)
    for h in range(2):
        line = flat_ref[h][:, HALF * half : HALF * (half + 1)].astype(f32)
        column = jnp.broadcast_to(line, (8, HALF)).T[:, :1].astype(jnp.int32)
        place = (slot == column).astype(f32).astype(bf16)
        rows = jnp.concatenate([in_ref[:, x, h].reshape(ROWS, WIDTH) for x in range(3)], axis=1)
        own_ref[:, 3 * WIDTH * h : 3 * WIDTH * (h + 1)] = dot(place, rows).astype(bf16)


def unpack(half, flat, home):
    return pl.pallas_call(
        functools.partial(unpack_kernel, half),
        in_specs=[WHOLE, WHOLE],
        out_specs=WHOLE,
        out_shape=pltpu.VMEM((HALF, 6 * WIDTH), bf16),
        compiler_params=pltpu.CompilerParams(vmem_limit_bytes=12 * MIB),
        name="unpack",
    )(flat, near(home))


def merge_kernel(a_ref, b_ref, q_ref, k_ref, v_ref):
    i, j = iota((256, 256), 0), iota((256, 256), 1)
    merge = (i == jnp.where(j < 128, 2 * j, 2 * j - 255)).astype(f32).astype(bf16)
    for s, ref in enumerate((a_ref, b_ref)):
        for b in range(HALF // 128):
            rows = ref[128 * b : 128 * (b + 1), :]
            both = jnp.concatenate([rows[:, : 3 * WIDTH], rows[:, 3 * WIDTH :]], axis=0)
            mixed = dot(merge, both).astype(bf16)
            at = 2 * HALF * s + 256 * b
            q_ref[at : at + 256, :] = mixed[:, :WIDTH]
            k_ref[at : at + 256, :] = mixed[:, WIDTH : 2 * WIDTH]
            v_ref[at : at + 256, :] = mixed[:, 2 * WIDTH :]


def merge(own_a, own_b):
    one = jax.ShapeDtypeStruct((2 * TOK, WIDTH), bf16)
    return pl.pallas_call(
        merge_kernel,
        in_specs=[WHOLE, WHOLE],
        out_specs=(WHOLE,) * 3,
        out_shape=(one, one, one),
        compiler_params=pltpu.CompilerParams(vmem_limit_bytes=6 * MIB),
        cost_estimate=pl.CostEstimate(flops=10**9, bytes_accessed=3 * 10**6, transcendentals=0),
        name="merge",
    )(near(own_a), near(own_b))


def project_kernel(plan, *refs):
    mine_ref, theirs_ref = refs[:2]
    grads, outs = refs[2 : len(refs) - len(plan)], refs[len(refs) - len(plan) :]
    for (at, j), out in zip(plan, outs):
        total = dot(grads[at][...], mine_ref[j]) + dot(grads[at + 1][...], theirs_ref[j])
        out[...] = total.astype(out.dtype)


def project(plan, types, mine, theirs, *grads):
    return pl.pallas_call(
        functools.partial(project_kernel, plan),
        in_specs=[WHOLE] * (2 + len(grads)),
        out_specs=(WHOLE,) * len(plan),
        out_shape=tuple(pltpu.VMEM((HALF, QUARTER), kind) for kind in types),
        compiler_params=pltpu.CompilerParams(vmem_limit_bytes=6 * MIB),
        cost_estimate=pl.CostEstimate(
            flops=len(plan) * 4 * HALF * QUARTER * 6 * WIDTH, bytes_accessed=10**6, transcendentals=0
        ),
        name="project",
    )(*[near(x) for x in (mine, theirs, *grads)])


def finish_kernel(a_ref, b_ref, a_up, a_down, b_up, b_down, out_ref):
    for s, (own, up, down) in enumerate(((a_ref, a_up, a_down), (b_ref, b_up, b_down))):
        total = own[...] + up[...].astype(f32) + down[...].astype(f32)
        out_ref[:, HALF * s : HALF * (s + 1)] = total.T.astype(bf16)


def finish(*parts):
    return pl.pallas_call(
        finish_kernel,
        in_specs=[WHOLE] * 6,
        out_specs=WHOLE,
        out_shape=jax.ShapeDtypeStruct((QUARTER, TOK), bf16),
        compiler_params=pltpu.CompilerParams(vmem_limit_bytes=6 * MIB),
        name="finish",
    )(*[near(x) for x in parts])


def shards(queries, keys, values, out_grad, cluster_ids, query_weight, key_weight, value_weight):
    place = lax.axis_index("head")
    core, z = place % 2, place // 2
    swap = [(i, i ^ 1) for i in range(8)]
    up = [(i, (i + 2) % 8) for i in range(8)]
    down = [(i, (i - 2) % 8) for i in range(8)]

    def blocks(which):
        parts = [w.reshape(4, 2, QUARTER, 2, WIDTH) for w in (query_weight, key_weight, value_weight)]
        parts = [lax.dynamic_index_in_dim(w, which, 1, keepdims=False) for w in parts]
        whole = jnp.transpose(jnp.stack(parts, axis=3), (0, 2, 3, 4, 1)).reshape(4, 6 * WIDTH, QUARTER)
        return jnp.roll(whole, -z, axis=0)

    mine = blocks(core)
    theirs = lax.ppermute(blocks(1 - core), "head", swap)

    ids = jnp.transpose(cluster_ids, (0, 2, 1))
    flat2 = [x.reshape(2 * TOK, WIDTH) for x in (queries, keys, values, out_grad)]
    sent, flat = pack(ids, *flat2)
    got = lax.all_to_all(sent, "seq", split_axis=0, concat_axis=0, tiled=True)
    back, sums = attend(got)
    key_sums = jnp.transpose(sums, (1, 0, 2))
    home = lax.all_to_all(back, "seq", split_axis=0, concat_axis=0, tiled=True)
    home, mine, theirs = lax.optimization_barrier((home, mine, theirs))
    own_a = unpack(0, flat, home)
    other_a = lax.ppermute(own_a, "head", swap)
    own_b = unpack(1, flat, home)
    other_b = lax.ppermute(own_b, "head", swap)

    far_a, down_a = project(((0, 2), (0, 3)), (bf16, bf16), mine, theirs, own_a, other_a)
    far_a = lax.ppermute(far_a, "head", up)
    down_a = lax.ppermute(down_a, "head", down)
    far_b, up_b = project(((0, 2), (0, 1)), (bf16, bf16), mine, theirs, own_b, other_b)
    far_b = lax.ppermute(far_b, "head", down)
    up_b = lax.ppermute(up_b, "head", up)
    next_a, last_b = project(
        ((0, 1), (2, 3)), (f32,) * 2, mine, theirs, own_a, other_a, own_b, other_b
    )
    up_a = lax.ppermute((next_a + far_a.astype(f32)).astype(bf16), "head", up)
    down_b = lax.ppermute((last_b + far_b.astype(f32)).astype(bf16), "head", down)
    own_sum_a, own_sum_b = project(
        ((0, 0), (2, 0)), (f32,) * 2, mine, theirs, own_a, other_a, own_b, other_b
    )
    input_grad = finish(own_sum_a, own_sum_b, up_a, down_a, up_b, down_b)
    grads = [x.reshape(TOK, 2, WIDTH) for x in merge(own_a, own_b)]
    return (*grads, input_grad, key_sums)


def solution(mesh):
    placed = (
        P("seq", "head", None),
        P("seq", "head", None),
        P("seq", "head", None),
        P("seq", "head", None),
        P("head", "seq", None),
        P(None, "head", None),
        P(None, "head", None),
        P(None, "head", None),
    )
    return jax.shard_map(
        shards,
        mesh=mesh,
        in_specs=placed,
        out_specs=(
            P("seq", "head", None),
            P("seq", "head", None),
            P("seq", "head", None),
            P("head", "seq"),
            P("head", "seq", None),
        ),
        check_vma=False,
    )
```

```python
import functools
import math

import jax
import jax.numpy as jnp
from jax import lax
from jax.experimental import pallas as pl
from jax.experimental.pallas import tpu as pltpu
from jax.sharding import PartitionSpec as P

CLUSTERS = 192
SLOTS = 8
WIDTH = 128
TOK = 1024
HALF = TOK // 2
SEQ = 16
CL_DEV = CLUSTERS // SEQ
RUN = CL_DEV * SLOTS
ROWS = CLUSTERS * SLOTS
QUARTER = 256
EMPTY = 1024.0
LIMIT = 100.0
PACK_DSTS = 2

f32 = jnp.float32
bf16 = jnp.bfloat16
WHOLE = pl.BlockSpec(memory_space=pltpu.VMEM)
MIB = 1024 * 1024


def near(x):
    return pltpu.with_memory_space_constraint(x, pltpu.VMEM)


def dot(a, b):
    return jnp.dot(a, b, preferred_element_type=f32)


def dot_nt(a, b):
    return lax.dot_general(a, b, (((1,), (1,)), ((), ())), preferred_element_type=f32)


def dot_tn(a, b):
    return lax.dot_general(a, b, (((0,), (0,)), ((), ())), preferred_element_type=f32)


def iota(shape, axis):
    return lax.broadcasted_iota(jnp.int32, shape, axis)


def pack_kernel(ids_ref, q_ref, k_ref, v_ref, g_ref, out_ref, flat_ref, pairs_ref, rows_ref, sem):
    copies = []
    for x, ref in enumerate((q_ref, k_ref, v_ref, g_ref)):
        copy = pltpu.make_async_copy(ref, pairs_ref.at[x], sem.at[x])
        copy.start()
        copies.append(copy)
    u, t = iota((256, 512), 0), iota((256, 512), 1)
    earlier = ((u < t) | (t >= 256)).astype(f32).astype(bf16)
    ids = [ids_ref[h] for h in range(2)]
    cluster = iota((CLUSTERS, 256), 0)
    carry = jnp.zeros((2 * CLUSTERS, 256), f32)
    ranks = [[], []]
    for b in range(TOK // 256):
        member = jnp.concatenate(
            [(cluster == line[:, 256 * b : 256 * (b + 1)]).astype(f32) for line in ids], axis=0
        )
        sums = dot(member.astype(bf16), earlier)
        mine = member * (sums[:, :256] + carry)
        carry = carry + sums[:, 256:]
        for h in range(2):
            part = mine[CLUSTERS * h : CLUSTERS * (h + 1)]
            ranks[h].append(jnp.sum(part, axis=0, keepdims=True))
    flats = []
    for h in range(2):
        flat = ids[h] * SLOTS + jnp.concatenate(ranks[h], axis=1).astype(jnp.int32)
        flat_ref[h] = flat
        flats.append(flat)
    for copy in copies:
        copy.wait()
    i, j = iota((256, 256), 0), iota((256, 256), 1)
    split = (j == jnp.where(i < 128, 2 * i, 2 * i - 255)).astype(f32).astype(bf16)
    for b in range(TOK // 128):
        block = jnp.concatenate([pairs_ref[x, 256 * b : 256 * (b + 1), :] for x in range(4)], axis=1)
        parted = dot(split, block).astype(bf16)
        rows_ref[0, 128 * b : 128 * (b + 1), :] = parted[:128]
        rows_ref[1, 128 * b : 128 * (b + 1), :] = parted[128:]
    step = PACK_DSTS * RUN
    slot = iota((step, TOK), 0)
    groups = (PACK_DSTS * CL_DEV, SLOTS, WIDTH)
    rank = iota(groups, 1).astype(f32)
    for j in range(SEQ // PACK_DSTS):
        for h in range(2):
            place = (slot == flats[h] - j * step).astype(f32).astype(bf16)
            moved = dot(place, rows_ref[h])
            for x in range(4):
                piece = moved[:, WIDTH * x : WIDTH * (x + 1)]
                if x == 1:
                    at = CLUSTERS * h + groups[0] * j
                    count = jnp.broadcast_to(carry[at : at + groups[0], None, :WIDTH], groups)
                    piece = jnp.where(rank < count, piece.reshape(groups), EMPTY)
                piece = piece.reshape(PACK_DSTS, RUN, WIDTH).astype(bf16)
                out_ref[PACK_DSTS * j : PACK_DSTS * (j + 1), x, h] = piece


def pack(ids, *tensors):
    far = [pltpu.with_memory_space_constraint(x, pltpu.HBM) for x in tensors]
    return pl.pallas_call(
        pack_kernel,
        in_specs=[WHOLE] + [pl.BlockSpec(memory_space=pltpu.HBM)] * 4,
        out_specs=(WHOLE, WHOLE),
        out_shape=(
            pltpu.VMEM((SEQ, 4, 2, RUN, WIDTH), bf16),
            jax.ShapeDtypeStruct((2, 1, TOK), jnp.int32),
        ),
        scratch_shapes=[
            pltpu.VMEM((4, 2 * TOK, WIDTH), bf16),
            pltpu.VMEM((2, TOK, 4 * WIDTH), bf16),
            pltpu.SemaphoreType.DMA((4,)),
        ],
        compiler_params=pltpu.CompilerParams(vmem_limit_bytes=16 * MIB),
        name="pack",
    )(ids, *far)


def attend_kernel(in_ref, back_ref, sums_ref, qkg_ref, pd_ref, out_ref, sem):
    scale = 1.0 / math.sqrt(WIDTH)
    count = SEQ * SLOTS
    key, query = iota((count, count), 0), iota((count, count), 1)
    causal, diagonal = key < query, key == query
    spots = [(h, c) for h in range(2) for c in range(0, CL_DEV, 2)]
    for h, c in spots:
        wide = [in_ref[:, x, h, SLOTS * c : SLOTS * (c + 2)].astype(f32) for x in range(4)]
        for s in range(2):
            q32, k32, v32, g32 = [
                w[:, SLOTS * s : SLOTS * (s + 1)].reshape(count, WIDTH) for w in wide
            ]
            q, k, v, g = (x.astype(bf16) for x in (q32, k32, v32, g32))
            for x, y in enumerate((q, k, g)):
                qkg_ref[h, c + s, x] = y
            empty = k32 > LIMIT
            total = jnp.sum(jnp.where(empty, 0.0, k32), axis=0, keepdims=True)
            sums_ref[c + s, h : h + 1] = total * scale
            allowed = (causal & jnp.logical_not(empty)) | diagonal
            score = jnp.where(allowed, dot_nt(k, q) * scale, -1e30)
            dprob = dot_nt(v, g)
            top = jnp.max(score, axis=0, keepdims=True)
            expo = jnp.exp(score - top)
            prob = expo * (1.0 / jnp.sum(expo, axis=0, keepdims=True))
            prob_b = prob.astype(bf16)
            delta = jnp.sum(prob_b.astype(f32) * dprob, axis=0, keepdims=True)
            pd_ref[h, c + s, 0] = prob_b
            pd_ref[h, c + s, 1] = (prob * (dprob - delta) * scale).astype(bf16)
    copies = []
    for h in range(2):
        for x in range(3):
            for c in range(0, CL_DEV, 2):
                halves = []
                for s in range(2):
                    first, second = pd_ref[h, c + s, 0 if x == 2 else 1], qkg_ref[h, c + s, (1, 0, 2)[x]]
                    grad = dot_tn(first, second) if x == 0 else dot(first, second)
                    halves.append(grad.reshape(SEQ, SLOTS, WIDTH))
                tile = jnp.concatenate(halves, axis=1).astype(bf16)
                out_ref[:, x, h, SLOTS * c : SLOTS * (c + 2)] = tile
            copy = pltpu.make_async_copy(out_ref.at[:, x, h], back_ref.at[:, x, h], sem.at[h, x])
            copy.start()
            copies.append(copy)
    for copy in copies:
        copy.wait()


def attend(got):
    return pl.pallas_call(
        attend_kernel,
        in_specs=[WHOLE],
        out_specs=(pl.BlockSpec(memory_space=pltpu.HBM), WHOLE),
        out_shape=(
            pltpu.HBM((SEQ, 3, 2, RUN, WIDTH), bf16),
            jax.ShapeDtypeStruct((CL_DEV, 2, WIDTH), f32),
        ),
        scratch_shapes=[
            pltpu.VMEM((2, CL_DEV, 3, SEQ * SLOTS, WIDTH), bf16),
            pltpu.VMEM((2, CL_DEV, 2, SEQ * SLOTS, SEQ * SLOTS), bf16),
            pltpu.VMEM((SEQ, 3, 2, RUN, WIDTH), bf16),
            pltpu.SemaphoreType.DMA((2, 3)),
        ],
        compiler_params=pltpu.CompilerParams(vmem_limit_bytes=12 * MIB),
        name="attend",
    )(near(got))


def gather(h, rows_ref, own_ref, place):
    rows = jnp.concatenate([rows_ref[h, x].reshape(ROWS, WIDTH) for x in range(3)], axis=1)
    own_ref[:, 3 * WIDTH * h : 3 * WIDTH * (h + 1)] = dot(place, rows).astype(bf16)


def places(half, h, flat_ref):
    slot = iota((HALF, ROWS), 1)
    line = flat_ref[h][:, HALF * half : HALF * (half + 1)].astype(f32)
    column = jnp.broadcast_to(line, (8, HALF)).T[:, :1].astype(jnp.int32)
    column = jnp.broadcast_to(column, slot.shape).astype(jnp.int16)
    return jnp.where(slot.astype(jnp.int16) == column, bf16(1), bf16(0))


def unpack_first_kernel(flat_ref, home_ref, own_ref, rows_ref, place_ref, sem):
    copies = []
    for h in range(2):
        for x in range(3):
            copy = pltpu.make_async_copy(home_ref.at[:, x, h], rows_ref.at[h, x], sem.at[h, x])
            copy.start()
            copies.append(copy)
    for h in range(2):
        place_ref[h] = places(1, h, flat_ref)
    for h in range(2):
        for copy in copies[3 * h : 3 * h + 3]:
            copy.wait()
        gather(h, rows_ref, own_ref, place_ref[h])


def unpack_first(flat, home):
    return pl.pallas_call(
        unpack_first_kernel,
        in_specs=[WHOLE, pl.BlockSpec(memory_space=pltpu.HBM)],
        out_specs=(WHOLE, WHOLE),
        out_shape=(
            pltpu.VMEM((HALF, 6 * WIDTH), bf16),
            pltpu.VMEM((2, 3, SEQ, RUN, WIDTH), bf16),
        ),
        scratch_shapes=[pltpu.VMEM((2, HALF, ROWS), bf16), pltpu.SemaphoreType.DMA((2, 3))],
        compiler_params=pltpu.CompilerParams(vmem_limit_bytes=16 * MIB),
        name="unpack_first",
    )(flat, pltpu.with_memory_space_constraint(home, pltpu.HBM))


def unpack_last_kernel(flat_ref, rows_ref, own_ref):
    for h in range(2):
        gather(h, rows_ref, own_ref, places(0, h, flat_ref))


def unpack_last(flat, rows):
    return pl.pallas_call(
        unpack_last_kernel,
        in_specs=[WHOLE, WHOLE],
        out_specs=WHOLE,
        out_shape=pltpu.VMEM((HALF, 6 * WIDTH), bf16),
        compiler_params=pltpu.CompilerParams(vmem_limit_bytes=12 * MIB),
        name="unpack_last",
    )(flat, near(rows))


def merge_kernel(a_ref, b_ref, q_ref, k_ref, v_ref):
    i, j = iota((256, 256), 0), iota((256, 256), 1)
    merge = (i == jnp.where(j < 128, 2 * j, 2 * j - 255)).astype(f32).astype(bf16)
    for s, ref in enumerate((a_ref, b_ref)):
        for b in range(HALF // 128):
            rows = ref[128 * b : 128 * (b + 1), :]
            both = jnp.concatenate([rows[:, : 3 * WIDTH], rows[:, 3 * WIDTH :]], axis=0)
            mixed = dot(merge, both).astype(bf16)
            at = 2 * HALF * s + 256 * b
            q_ref[at : at + 256, :] = mixed[:, :WIDTH]
            k_ref[at : at + 256, :] = mixed[:, WIDTH : 2 * WIDTH]
            v_ref[at : at + 256, :] = mixed[:, 2 * WIDTH :]


def merge(own_a, own_b):
    one = jax.ShapeDtypeStruct((2 * TOK, WIDTH), bf16)
    return pl.pallas_call(
        merge_kernel,
        in_specs=[WHOLE, WHOLE],
        out_specs=(WHOLE,) * 3,
        out_shape=(one, one, one),
        compiler_params=pltpu.CompilerParams(vmem_limit_bytes=6 * MIB),
        cost_estimate=pl.CostEstimate(flops=10**9, bytes_accessed=3 * 10**6, transcendentals=0),
        name="merge",
    )(near(own_a), near(own_b))


def project_kernel(plan, *refs):
    mine_ref, theirs_ref = refs[:2]
    grads, outs = refs[2 : len(refs) - len(plan)], refs[len(refs) - len(plan) :]
    for (at, j), out in zip(plan, outs):
        total = dot(grads[at][...], mine_ref[j]) + dot(grads[at + 1][...], theirs_ref[j])
        out[...] = total.astype(out.dtype)


def project(plan, types, mine, theirs, *grads):
    return pl.pallas_call(
        functools.partial(project_kernel, plan),
        in_specs=[WHOLE] * (2 + len(grads)),
        out_specs=(WHOLE,) * len(plan),
        out_shape=tuple(pltpu.VMEM((HALF, QUARTER), kind) for kind in types),
        compiler_params=pltpu.CompilerParams(vmem_limit_bytes=6 * MIB),
        cost_estimate=pl.CostEstimate(
            flops=len(plan) * 4 * HALF * QUARTER * 6 * WIDTH, bytes_accessed=10**6, transcendentals=0
        ),
        name="project",
    )(*[near(x) for x in (mine, theirs, *grads)])


def finish_kernel(a_ref, b_ref, a_up, a_down, b_up, b_down, out_ref):
    for s, (own, up, down) in enumerate(((a_ref, a_up, a_down), (b_ref, b_up, b_down))):
        total = own[...] + up[...].astype(f32) + down[...].astype(f32)
        out_ref[:, HALF * s : HALF * (s + 1)] = total.T.astype(bf16)


def finish(*parts):
    return pl.pallas_call(
        finish_kernel,
        in_specs=[WHOLE] * 6,
        out_specs=WHOLE,
        out_shape=jax.ShapeDtypeStruct((QUARTER, TOK), bf16),
        compiler_params=pltpu.CompilerParams(vmem_limit_bytes=6 * MIB),
        name="finish",
    )(*[near(x) for x in parts])


def shards(queries, keys, values, out_grad, cluster_ids, query_weight, key_weight, value_weight):
    place = lax.axis_index("head")
    core, z = place % 2, place // 2
    swap = [(i, i ^ 1) for i in range(8)]
    up = [(i, (i + 2) % 8) for i in range(8)]
    down = [(i, (i - 2) % 8) for i in range(8)]

    def blocks(which):
        parts = [w.reshape(4, 2, QUARTER, 2, WIDTH) for w in (query_weight, key_weight, value_weight)]
        parts = [lax.dynamic_index_in_dim(w, which, 1, keepdims=False) for w in parts]
        whole = jnp.transpose(jnp.stack(parts, axis=3), (0, 2, 3, 4, 1)).reshape(4, 6 * WIDTH, QUARTER)
        return jnp.roll(whole, -z, axis=0)

    mine = blocks(core)
    theirs = lax.ppermute(blocks(1 - core), "head", swap)

    ids = jnp.transpose(cluster_ids, (0, 2, 1))
    flat2 = [x.reshape(2 * TOK, WIDTH) for x in (queries, keys, values, out_grad)]
    sent, flat = pack(ids, *flat2)
    got = lax.all_to_all(sent, "seq", split_axis=0, concat_axis=0, tiled=True)
    back, sums = attend(got)
    key_sums = jnp.transpose(sums, (1, 0, 2))
    home = lax.all_to_all(back, "seq", split_axis=0, concat_axis=0, tiled=True)
    flat, mine, theirs = lax.optimization_barrier((flat, mine, theirs))
    own_b, rows = unpack_first(flat, home)
    other_b = lax.ppermute(own_b, "head", swap)
    own_a = unpack_last(flat, rows)
    other_a = lax.ppermute(own_a, "head", swap)

    far_a, down_a = project(((0, 2), (0, 3)), (bf16, bf16), mine, theirs, own_a, other_a)
    far_a = lax.ppermute(far_a, "head", up)
    down_a = lax.ppermute(down_a, "head", down)
    far_b, up_b = project(((0, 2), (0, 1)), (bf16, bf16), mine, theirs, own_b, other_b)
    far_b = lax.ppermute(far_b, "head", down)
    up_b = lax.ppermute(up_b, "head", up)
    next_a, last_b = project(
        ((0, 1), (2, 3)), (f32,) * 2, mine, theirs, own_a, other_a, own_b, other_b
    )
    up_a = lax.ppermute((next_a + far_a.astype(f32)).astype(bf16), "head", up)
    down_b = lax.ppermute((last_b + far_b.astype(f32)).astype(bf16), "head", down)
    own_sum_a, own_sum_b = project(
        ((0, 0), (2, 0)), (f32,) * 2, mine, theirs, own_a, other_a, own_b, other_b
    )
    input_grad = finish(own_sum_a, own_sum_b, up_a, down_a, up_b, down_b)
    grads = [x.reshape(TOK, 2, WIDTH) for x in merge(own_a, own_b)]
    return (*grads, input_grad, key_sums)


def solution(mesh):
    placed = (
        P("seq", "head", None),
        P("seq", "head", None),
        P("seq", "head", None),
        P("seq", "head", None),
        P("head", "seq", None),
        P(None, "head", None),
        P(None, "head", None),
        P(None, "head", None),
    )
    return jax.shard_map(
        shards,
        mesh=mesh,
        in_specs=placed,
        out_specs=(
            P("seq", "head", None),
            P("seq", "head", None),
            P("seq", "head", None),
            P("head", "seq"),
            P("head", "seq", None),
        ),
        check_vma=False,
    )
```

```python
import functools
import math

import jax
import jax.numpy as jnp
from jax import lax
from jax.experimental import pallas as pl
from jax.experimental.pallas import tpu as pltpu
from jax.sharding import PartitionSpec as P

CLUSTERS = 192
SLOTS = 8
WIDTH = 128
TOK = 1024
HALF = TOK // 2
SEQ = 16
CL_DEV = CLUSTERS // SEQ
RUN = CL_DEV * SLOTS
ROWS = CLUSTERS * SLOTS
QUARTER = 256
EMPTY = 1024.0
LIMIT = 100.0
PACK_DSTS = 2

f32 = jnp.float32
bf16 = jnp.bfloat16
WHOLE = pl.BlockSpec(memory_space=pltpu.VMEM)
MIB = 1024 * 1024


def near(x):
    return pltpu.with_memory_space_constraint(x, pltpu.VMEM)


def dot(a, b):
    return jnp.dot(a, b, preferred_element_type=f32)


def dot_nt(a, b):
    return lax.dot_general(a, b, (((1,), (1,)), ((), ())), preferred_element_type=f32)


def dot_tn(a, b):
    return lax.dot_general(a, b, (((0,), (0,)), ((), ())), preferred_element_type=f32)


def iota(shape, axis):
    return lax.broadcasted_iota(jnp.int32, shape, axis)


def pack_kernel(ids_ref, q_ref, k_ref, v_ref, g_ref, out_ref, flat_ref, pairs_ref, rows_ref, sem):
    copies = []
    for x, ref in enumerate((q_ref, k_ref, v_ref, g_ref)):
        copy = pltpu.make_async_copy(ref, pairs_ref.at[x], sem.at[x])
        copy.start()
        copies.append(copy)
    u, t = iota((256, 512), 0), iota((256, 512), 1)
    earlier = ((u < t) | (t >= 256)).astype(f32).astype(bf16)
    ids = [ids_ref[h] for h in range(2)]
    cluster = iota((CLUSTERS, 256), 0)
    carry = jnp.zeros((2 * CLUSTERS, 256), f32)
    ranks = [[], []]
    for b in range(TOK // 256):
        member = jnp.concatenate(
            [(cluster == line[:, 256 * b : 256 * (b + 1)]).astype(f32) for line in ids], axis=0
        )
        sums = dot(member.astype(bf16), earlier)
        mine = member * (sums[:, :256] + carry)
        carry = carry + sums[:, 256:]
        for h in range(2):
            part = mine[CLUSTERS * h : CLUSTERS * (h + 1)]
            ranks[h].append(jnp.sum(part, axis=0, keepdims=True))
    flats = []
    for h in range(2):
        flat = ids[h] * SLOTS + jnp.concatenate(ranks[h], axis=1).astype(jnp.int32)
        flat_ref[h] = flat
        flats.append(flat)
    for copy in copies:
        copy.wait()
    i, j = iota((256, 256), 0), iota((256, 256), 1)
    split = (j == jnp.where(i < 128, 2 * i, 2 * i - 255)).astype(f32).astype(bf16)
    for b in range(TOK // 128):
        block = jnp.concatenate([pairs_ref[x, 256 * b : 256 * (b + 1), :] for x in range(4)], axis=1)
        parted = dot(split, block).astype(bf16)
        rows_ref[0, 128 * b : 128 * (b + 1), :] = parted[:128]
        rows_ref[1, 128 * b : 128 * (b + 1), :] = parted[128:]
    step = PACK_DSTS * RUN
    slot = iota((step, TOK), 0)
    groups = (PACK_DSTS * CL_DEV, SLOTS, WIDTH)
    rank = iota(groups, 1).astype(f32)
    for j in range(SEQ // PACK_DSTS):
        for h in range(2):
            place = (slot == flats[h] - j * step).astype(f32).astype(bf16)
            moved = dot(place, rows_ref[h])
            for x in range(4):
                piece = moved[:, WIDTH * x : WIDTH * (x + 1)]
                if x == 1:
                    at = CLUSTERS * h + groups[0] * j
                    count = jnp.broadcast_to(carry[at : at + groups[0], None, :WIDTH], groups)
                    piece = jnp.where(rank < count, piece.reshape(groups), EMPTY)
                piece = piece.reshape(PACK_DSTS, RUN, WIDTH).astype(bf16)
                out_ref[PACK_DSTS * j : PACK_DSTS * (j + 1), x, h] = piece


def pack(ids, *tensors):
    far = [pltpu.with_memory_space_constraint(x, pltpu.HBM) for x in tensors]
    return pl.pallas_call(
        pack_kernel,
        in_specs=[WHOLE] + [pl.BlockSpec(memory_space=pltpu.HBM)] * 4,
        out_specs=(WHOLE, WHOLE),
        out_shape=(
            pltpu.VMEM((SEQ, 4, 2, RUN, WIDTH), bf16),
            jax.ShapeDtypeStruct((2, 1, TOK), jnp.int32),
        ),
        scratch_shapes=[
            pltpu.VMEM((4, 2 * TOK, WIDTH), bf16),
            pltpu.VMEM((2, TOK, 4 * WIDTH), bf16),
            pltpu.SemaphoreType.DMA((4,)),
        ],
        compiler_params=pltpu.CompilerParams(vmem_limit_bytes=16 * MIB),
        name="pack",
    )(ids, *far)


def attend_kernel(in_ref, back_ref, sums_ref, qkg_ref, pd_ref, out_ref, sem):
    scale = 1.0 / math.sqrt(WIDTH)
    count = SEQ * SLOTS
    key, query = iota((count, count), 0), iota((count, count), 1)
    causal, diagonal = key < query, key == query
    spots = [(h, c) for h in range(2) for c in range(0, CL_DEV, 2)]
    for h, c in spots:
        wide = [in_ref[:, x, h, SLOTS * c : SLOTS * (c + 2)].astype(f32) for x in range(4)]
        for s in range(2):
            q32, k32, v32, g32 = [
                w[:, SLOTS * s : SLOTS * (s + 1)].reshape(count, WIDTH) for w in wide
            ]
            q, k, v, g = (x.astype(bf16) for x in (q32, k32, v32, g32))
            for x, y in enumerate((q, k, g)):
                qkg_ref[h, c + s, x] = y
            empty = k32 > LIMIT
            total = jnp.sum(jnp.where(empty, 0.0, k32), axis=0, keepdims=True)
            sums_ref[c + s, h : h + 1] = total * scale
            allowed = (causal & jnp.logical_not(empty)) | diagonal
            score = jnp.where(allowed, dot_nt(k, q) * scale, -1e30)
            dprob = dot_nt(v, g)
            top = jnp.max(score, axis=0, keepdims=True)
            expo = jnp.exp(score - top)
            prob = expo * (1.0 / jnp.sum(expo, axis=0, keepdims=True))
            prob_b = prob.astype(bf16)
            delta = jnp.sum(prob_b.astype(f32) * dprob, axis=0, keepdims=True)
            pd_ref[h, c + s, 0] = prob_b
            pd_ref[h, c + s, 1] = (prob * (dprob - delta) * scale).astype(bf16)
    copies = []
    for h in range(2):
        for x in range(3):
            for c in range(0, CL_DEV, 2):
                halves = []
                for s in range(2):
                    first, second = pd_ref[h, c + s, 0 if x == 2 else 1], qkg_ref[h, c + s, (1, 0, 2)[x]]
                    grad = dot_tn(first, second) if x == 0 else dot(first, second)
                    halves.append(grad.reshape(SEQ, SLOTS, WIDTH))
                tile = jnp.concatenate(halves, axis=1).astype(bf16)
                out_ref[:, x, h, SLOTS * c : SLOTS * (c + 2)] = tile
            copy = pltpu.make_async_copy(out_ref.at[:, x, h], back_ref.at[:, x, h], sem.at[h, x])
            copy.start()
            copies.append(copy)
    for copy in copies:
        copy.wait()


def attend(got):
    return pl.pallas_call(
        attend_kernel,
        in_specs=[WHOLE],
        out_specs=(pl.BlockSpec(memory_space=pltpu.HBM), WHOLE),
        out_shape=(
            pltpu.HBM((SEQ, 3, 2, RUN, WIDTH), bf16),
            jax.ShapeDtypeStruct((CL_DEV, 2, WIDTH), f32),
        ),
        scratch_shapes=[
            pltpu.VMEM((2, CL_DEV, 3, SEQ * SLOTS, WIDTH), bf16),
            pltpu.VMEM((2, CL_DEV, 2, SEQ * SLOTS, SEQ * SLOTS), bf16),
            pltpu.VMEM((SEQ, 3, 2, RUN, WIDTH), bf16),
            pltpu.SemaphoreType.DMA((2, 3)),
        ],
        compiler_params=pltpu.CompilerParams(vmem_limit_bytes=12 * MIB),
        name="attend",
    )(near(got))


def gather(h, rows_ref, own_ref, place):
    rows = jnp.concatenate([rows_ref[h, x].reshape(ROWS, WIDTH) for x in range(3)], axis=1)
    own_ref[:, 3 * WIDTH * h : 3 * WIDTH * (h + 1)] = dot(place, rows).astype(bf16)


def places(half, h, flat_ref):
    slot = iota((HALF, ROWS), 1)
    line = flat_ref[h][:, HALF * half : HALF * (half + 1)].astype(f32)
    column = jnp.broadcast_to(line, (8, HALF)).T[:, :1].astype(jnp.int32)
    column = jnp.broadcast_to(column, slot.shape).astype(jnp.int16)
    return jnp.where(slot.astype(jnp.int16) == column, bf16(1), bf16(0))


def unpack_first_kernel(flat_ref, home_ref, own_ref, rows_ref, place_ref, sem):
    copies = []
    for h in range(2):
        for x in range(3):
            copy = pltpu.make_async_copy(home_ref.at[:, x, h], rows_ref.at[h, x], sem.at[h, x])
            copy.start()
            copies.append(copy)
    for h in range(2):
        place_ref[h] = places(0, h, flat_ref)
    for h in range(2):
        for copy in copies[3 * h : 3 * h + 3]:
            copy.wait()
        gather(h, rows_ref, own_ref, place_ref[h])


def unpack_first(flat, home):
    return pl.pallas_call(
        unpack_first_kernel,
        in_specs=[WHOLE, pl.BlockSpec(memory_space=pltpu.HBM)],
        out_specs=(WHOLE, WHOLE),
        out_shape=(
            pltpu.VMEM((HALF, 6 * WIDTH), bf16),
            pltpu.VMEM((2, 3, SEQ, RUN, WIDTH), bf16),
        ),
        scratch_shapes=[pltpu.VMEM((2, HALF, ROWS), bf16), pltpu.SemaphoreType.DMA((2, 3))],
        compiler_params=pltpu.CompilerParams(vmem_limit_bytes=16 * MIB),
        name="unpack_first",
    )(flat, pltpu.with_memory_space_constraint(home, pltpu.HBM))


def unpack_last_kernel(flat_ref, rows_ref, own_ref):
    for h in range(2):
        gather(h, rows_ref, own_ref, places(1, h, flat_ref))


def unpack_last(flat, rows):
    return pl.pallas_call(
        unpack_last_kernel,
        in_specs=[WHOLE, WHOLE],
        out_specs=WHOLE,
        out_shape=pltpu.VMEM((HALF, 6 * WIDTH), bf16),
        compiler_params=pltpu.CompilerParams(vmem_limit_bytes=12 * MIB),
        name="unpack_last",
    )(flat, near(rows))


def merge_kernel(a_ref, b_ref, q_ref, k_ref, v_ref):
    i, j = iota((256, 256), 0), iota((256, 256), 1)
    merge = (i == jnp.where(j < 128, 2 * j, 2 * j - 255)).astype(f32).astype(bf16)
    for s, ref in enumerate((a_ref, b_ref)):
        for b in range(HALF // 128):
            rows = ref[128 * b : 128 * (b + 1), :]
            both = jnp.concatenate([rows[:, : 3 * WIDTH], rows[:, 3 * WIDTH :]], axis=0)
            mixed = dot(merge, both).astype(bf16)
            at = 2 * HALF * s + 256 * b
            q_ref[at : at + 256, :] = mixed[:, :WIDTH]
            k_ref[at : at + 256, :] = mixed[:, WIDTH : 2 * WIDTH]
            v_ref[at : at + 256, :] = mixed[:, 2 * WIDTH :]


def merge(own_a, own_b):
    one = jax.ShapeDtypeStruct((2 * TOK, WIDTH), bf16)
    return pl.pallas_call(
        merge_kernel,
        in_specs=[WHOLE, WHOLE],
        out_specs=(WHOLE,) * 3,
        out_shape=(one, one, one),
        compiler_params=pltpu.CompilerParams(vmem_limit_bytes=6 * MIB),
        cost_estimate=pl.CostEstimate(flops=10**9, bytes_accessed=3 * 10**6, transcendentals=0),
        name="merge",
    )(near(own_a), near(own_b))


def project_kernel(plan, count, skip, *refs):
    mine_ref, theirs_ref = refs[:2]
    outs = refs[-len(plan) :]
    grads, extra = refs[2 : 2 + count], refs[2 + count : -len(plan) - skip]
    for i, ((at, j), out) in enumerate(zip(plan, outs)):
        total = dot(grads[at][...], mine_ref[j]) + dot(grads[at + 1][...], theirs_ref[j])
        if extra and i == len(plan) - 1:
            total = total + extra[0][...].astype(f32)
        out[...] = total.astype(out.dtype)


def project(plan, types, mine, theirs, grads, extra=(), after=()):
    return pl.pallas_call(
        functools.partial(project_kernel, plan, len(grads), len(after)),
        in_specs=[WHOLE] * (2 + len(grads) + len(extra)) + [pl.BlockSpec(memory_space=pl.ANY)] * len(after),
        out_specs=(WHOLE,) * len(plan),
        out_shape=tuple(pltpu.VMEM((HALF, QUARTER), kind) for kind in types),
        compiler_params=pltpu.CompilerParams(vmem_limit_bytes=6 * MIB),
        cost_estimate=pl.CostEstimate(
            flops=len(plan) * 4 * HALF * QUARTER * 6 * WIDTH, bytes_accessed=10**6, transcendentals=0
        ),
        name="project",
    )(*[near(x) for x in (mine, theirs, *grads, *extra)], *after)


def finish_kernel(a_ref, b_ref, a_up, b_down, out_ref):
    for s, (own, got) in enumerate(((a_ref, a_up), (b_ref, b_down))):
        total = own[...] + got[...].astype(f32)
        out_ref[:, HALF * s : HALF * (s + 1)] = total.T.astype(bf16)


def finish(*parts):
    return pl.pallas_call(
        finish_kernel,
        in_specs=[WHOLE] * 4,
        out_specs=WHOLE,
        out_shape=jax.ShapeDtypeStruct((QUARTER, TOK), bf16),
        compiler_params=pltpu.CompilerParams(vmem_limit_bytes=6 * MIB),
        name="finish",
    )(*[near(x) for x in parts])


def shards(queries, keys, values, out_grad, cluster_ids, query_weight, key_weight, value_weight):
    place = lax.axis_index("head")
    core, z = place % 2, place // 2
    swap = [(i, i ^ 1) for i in range(8)]
    up = [(i, (i + 2) % 8) for i in range(8)]
    down = [(i, (i - 2) % 8) for i in range(8)]

    def blocks(which):
        parts = [w.reshape(4, 2, QUARTER, 2, WIDTH) for w in (query_weight, key_weight, value_weight)]
        parts = [lax.dynamic_index_in_dim(w, which, 1, keepdims=False) for w in parts]
        whole = jnp.transpose(jnp.stack(parts, axis=3), (0, 2, 3, 4, 1)).reshape(4, 6 * WIDTH, QUARTER)
        return jnp.roll(whole, -z, axis=0)

    mine = blocks(core)
    theirs = lax.ppermute(blocks(1 - core), "head", swap)

    ids = jnp.transpose(cluster_ids, (0, 2, 1))
    flat2 = [x.reshape(2 * TOK, WIDTH) for x in (queries, keys, values, out_grad)]
    sent, flat = pack(ids, *flat2)
    got = lax.all_to_all(sent, "seq", split_axis=0, concat_axis=0, tiled=True)
    back, sums = attend(got)
    key_sums = jnp.transpose(sums, (1, 0, 2))
    home = lax.all_to_all(back, "seq", split_axis=0, concat_axis=0, tiled=True)
    flat, mine, theirs = lax.optimization_barrier((flat, mine, theirs))
    own_a, rows = unpack_first(flat, home)
    other_a = lax.ppermute(own_a, "head", swap)
    own_b = unpack_last(flat, rows)
    other_b = lax.ppermute(own_b, "head", swap)

    half_a, half_b = (own_a, other_a), (own_b, other_b)
    first, second = project(((0, 2), (0, 3)), (bf16, bf16), mine, theirs, half_a)
    far_a = lax.ppermute(first, "head", up)
    down_a = lax.ppermute(second, "head", down)
    far_b, up_b = project(((0, 2), (0, 1)), (bf16, bf16), mine, theirs, half_b, after=(first,))
    far_b = lax.ppermute(far_b, "head", down)
    up_b = lax.ppermute(up_b, "head", up)
    (last_b,) = project(((0, 3),), (f32,), mine, theirs, half_b)
    (sum_b,) = project(((0, 0),), (f32,), mine, theirs, half_b, (up_b,))
    down_b = lax.ppermute((last_b + far_b.astype(f32)).astype(bf16), "head", down)
    (next_a,) = project(((0, 1),), (f32,), mine, theirs, half_a)
    (sum_a,) = project(((0, 0),), (f32,), mine, theirs, half_a, (down_a,))
    up_a = lax.ppermute((next_a + far_a.astype(f32)).astype(bf16), "head", up)
    input_grad = finish(sum_a, sum_b, up_a, down_b)
    grads = [x.reshape(TOK, 2, WIDTH) for x in merge(own_a, own_b)]
    return (*grads, input_grad, key_sums)


def solution(mesh):
    placed = (
        P("seq", "head", None),
        P("seq", "head", None),
        P("seq", "head", None),
        P("seq", "head", None),
        P("head", "seq", None),
        P(None, "head", None),
        P(None, "head", None),
        P(None, "head", None),
    )
    return jax.shard_map(
        shards,
        mesh=mesh,
        in_specs=placed,
        out_specs=(
            P("seq", "head", None),
            P("seq", "head", None),
            P("seq", "head", None),
            P("head", "seq"),
            P("head", "seq", None),
        ),
        check_vma=False,
    )
```

```python
import functools
import math

import jax
import jax.numpy as jnp
from jax import lax
from jax.experimental import pallas as pl
from jax.experimental.pallas import tpu as pltpu
from jax.sharding import PartitionSpec as P

CLUSTERS = 192
SLOTS = 8
WIDTH = 128
TOK = 1024
HALF = TOK // 2
SEQ = 16
CL_DEV = CLUSTERS // SEQ
RUN = CL_DEV * SLOTS
ROWS = CLUSTERS * SLOTS
QUARTER = 256
EMPTY = 1024.0
LIMIT = 100.0
PACK_DSTS = 2

f32 = jnp.float32
bf16 = jnp.bfloat16
WHOLE = pl.BlockSpec(memory_space=pltpu.VMEM)
MIB = 1024 * 1024


def near(x):
    return pltpu.with_memory_space_constraint(x, pltpu.VMEM)


def dot(a, b):
    return jnp.dot(a, b, preferred_element_type=f32)


def dot_nt(a, b):
    return lax.dot_general(a, b, (((1,), (1,)), ((), ())), preferred_element_type=f32)


def dot_tn(a, b):
    return lax.dot_general(a, b, (((0,), (0,)), ((), ())), preferred_element_type=f32)


def iota(shape, axis):
    return lax.broadcasted_iota(jnp.int32, shape, axis)


def pack_kernel(ids_ref, q_ref, k_ref, v_ref, g_ref, out_ref, flat_ref, pairs_ref, rows_ref, sem):
    copies = []
    for x, ref in enumerate((q_ref, k_ref, v_ref, g_ref)):
        copy = pltpu.make_async_copy(ref, pairs_ref.at[x], sem.at[x])
        copy.start()
        copies.append(copy)
    u, t = iota((256, 512), 0), iota((256, 512), 1)
    earlier = ((u < t) | (t >= 256)).astype(f32).astype(bf16)
    ids = [ids_ref[h] for h in range(2)]
    cluster = iota((CLUSTERS, 256), 0)
    carry = jnp.zeros((2 * CLUSTERS, 256), f32)
    ranks = [[], []]
    for b in range(TOK // 256):
        member = jnp.concatenate(
            [(cluster == line[:, 256 * b : 256 * (b + 1)]).astype(f32) for line in ids], axis=0
        )
        sums = dot(member.astype(bf16), earlier)
        mine = member * (sums[:, :256] + carry)
        carry = carry + sums[:, 256:]
        for h in range(2):
            part = mine[CLUSTERS * h : CLUSTERS * (h + 1)]
            ranks[h].append(jnp.sum(part, axis=0, keepdims=True))
    flats = []
    for h in range(2):
        flat = ids[h] * SLOTS + jnp.concatenate(ranks[h], axis=1).astype(jnp.int32)
        flat_ref[h] = flat
        flats.append(flat)
    i, j = iota((256, 256), 0), iota((256, 256), 1)
    split = (j == jnp.where(i < 128, 2 * i, 2 * i - 255)).astype(f32).astype(bf16)
    for x in (0, 2):
        copies[x].wait()
        copies[x + 1].wait()
        for b in range(TOK // 128):
            block = jnp.concatenate(
                [pairs_ref[y, 256 * b : 256 * (b + 1), :] for y in (x, x + 1)], axis=1
            )
            parted = dot(split, block).astype(bf16)
            at = slice(WIDTH * x, WIDTH * (x + 2))
            rows_ref[0, 128 * b : 128 * (b + 1), at] = parted[:128]
            rows_ref[1, 128 * b : 128 * (b + 1), at] = parted[128:]
    step = PACK_DSTS * RUN
    slot = iota((step, TOK), 0)
    groups = (PACK_DSTS * CL_DEV, SLOTS, WIDTH)
    rank = iota(groups, 1).astype(f32)
    for j in range(SEQ // PACK_DSTS):
        for h in range(2):
            place = (slot == flats[h] - j * step).astype(f32).astype(bf16)
            moved = dot(place, rows_ref[h])
            for x in range(4):
                piece = moved[:, WIDTH * x : WIDTH * (x + 1)]
                if x == 1:
                    at = CLUSTERS * h + groups[0] * j
                    count = jnp.broadcast_to(carry[at : at + groups[0], None, :WIDTH], groups)
                    piece = jnp.where(rank < count, piece.reshape(groups), EMPTY)
                piece = piece.reshape(PACK_DSTS, RUN, WIDTH).astype(bf16)
                out_ref[PACK_DSTS * j : PACK_DSTS * (j + 1), x, h] = piece


def pack(ids, *tensors):
    far = [pltpu.with_memory_space_constraint(x, pltpu.HBM) for x in tensors]
    return pl.pallas_call(
        pack_kernel,
        in_specs=[WHOLE] + [pl.BlockSpec(memory_space=pltpu.HBM)] * 4,
        out_specs=(WHOLE, WHOLE),
        out_shape=(
            pltpu.VMEM((SEQ, 4, 2, RUN, WIDTH), bf16),
            jax.ShapeDtypeStruct((2, 1, TOK), jnp.int32),
        ),
        scratch_shapes=[
            pltpu.VMEM((4, 2 * TOK, WIDTH), bf16),
            pltpu.VMEM((2, TOK, 4 * WIDTH), bf16),
            pltpu.SemaphoreType.DMA((4,)),
        ],
        compiler_params=pltpu.CompilerParams(vmem_limit_bytes=16 * MIB),
        name="pack",
    )(ids, *far)


def attend_kernel(in_ref, back_ref, sums_ref, qkg_ref, pd_ref, out_ref, sem):
    scale = 1.0 / math.sqrt(WIDTH)
    count = SEQ * SLOTS
    key, query = iota((count, count), 0), iota((count, count), 1)
    causal, diagonal = key < query, key == query
    spots = [(h, c) for h in range(2) for c in range(0, CL_DEV, 2)]
    for h, c in spots:
        wide = [in_ref[:, x, h, SLOTS * c : SLOTS * (c + 2)].astype(f32) for x in range(4)]
        for s in range(2):
            q32, k32, v32, g32 = [
                w[:, SLOTS * s : SLOTS * (s + 1)].reshape(count, WIDTH) for w in wide
            ]
            q, k, v, g = (x.astype(bf16) for x in (q32, k32, v32, g32))
            for x, y in enumerate((q, k, g)):
                qkg_ref[h, c + s, x] = y
            empty = k32 > LIMIT
            total = jnp.sum(jnp.where(empty, 0.0, k32), axis=0, keepdims=True)
            sums_ref[c + s, h : h + 1] = total * scale
            allowed = (causal & jnp.logical_not(empty)) | diagonal
            score = jnp.where(allowed, dot_nt(k, q) * scale, -1e30)
            dprob = dot_nt(v, g)
            top = jnp.max(score, axis=0, keepdims=True)
            expo = jnp.exp(score - top)
            prob = expo * (1.0 / jnp.sum(expo, axis=0, keepdims=True))
            prob_b = prob.astype(bf16)
            delta = jnp.sum(prob_b.astype(f32) * dprob, axis=0, keepdims=True)
            pd_ref[h, c + s, 0] = prob_b
            pd_ref[h, c + s, 1] = (prob * (dprob - delta) * scale).astype(bf16)
    copies = []
    for h in range(2):
        for x in range(3):
            for c in range(0, CL_DEV, 2):
                halves = []
                for s in range(2):
                    first, second = pd_ref[h, c + s, 0 if x == 2 else 1], qkg_ref[h, c + s, (1, 0, 2)[x]]
                    grad = dot_tn(first, second) if x == 0 else dot(first, second)
                    halves.append(grad.reshape(SEQ, SLOTS, WIDTH))
                tile = jnp.concatenate(halves, axis=1).astype(bf16)
                out_ref[:, x, h, SLOTS * c : SLOTS * (c + 2)] = tile
            copy = pltpu.make_async_copy(out_ref.at[:, x, h], back_ref.at[:, x, h], sem.at[h, x])
            copy.start()
            copies.append(copy)
    for copy in copies:
        copy.wait()


def attend(got):
    return pl.pallas_call(
        attend_kernel,
        in_specs=[WHOLE],
        out_specs=(pl.BlockSpec(memory_space=pltpu.HBM), WHOLE),
        out_shape=(
            pltpu.HBM((SEQ, 3, 2, RUN, WIDTH), bf16),
            jax.ShapeDtypeStruct((CL_DEV, 2, WIDTH), f32),
        ),
        scratch_shapes=[
            pltpu.VMEM((2, CL_DEV, 3, SEQ * SLOTS, WIDTH), bf16),
            pltpu.VMEM((2, CL_DEV, 2, SEQ * SLOTS, SEQ * SLOTS), bf16),
            pltpu.VMEM((SEQ, 3, 2, RUN, WIDTH), bf16),
            pltpu.SemaphoreType.DMA((2, 3)),
        ],
        compiler_params=pltpu.CompilerParams(vmem_limit_bytes=12 * MIB),
        name="attend",
    )(near(got))


def gather(h, rows_ref, own_ref, place):
    rows = jnp.concatenate([rows_ref[h, x].reshape(ROWS, WIDTH) for x in range(3)], axis=1)
    own_ref[:, 3 * WIDTH * h : 3 * WIDTH * (h + 1)] = dot(place, rows).astype(bf16)


def places(half, h, flat_ref):
    slot = iota((HALF, ROWS), 1)
    line = flat_ref[h][:, HALF * half : HALF * (half + 1)].astype(f32)
    column = jnp.broadcast_to(line, (8, HALF)).T[:, :1].astype(jnp.int32)
    column = jnp.broadcast_to(column, slot.shape).astype(jnp.int16)
    return jnp.where(slot.astype(jnp.int16) == column, bf16(1), bf16(0))


def unpack_first_kernel(flat_ref, home_ref, own_ref, rows_ref, place_ref, sem):
    copies = []
    for h in range(2):
        for x in range(3):
            copy = pltpu.make_async_copy(home_ref.at[:, x, h], rows_ref.at[h, x], sem.at[h, x])
            copy.start()
            copies.append(copy)
    for h in range(2):
        place_ref[h] = places(0, h, flat_ref)
    for h in range(2):
        for copy in copies[3 * h : 3 * h + 3]:
            copy.wait()
        gather(h, rows_ref, own_ref, place_ref[h])


def unpack_first(flat, home):
    return pl.pallas_call(
        unpack_first_kernel,
        in_specs=[WHOLE, pl.BlockSpec(memory_space=pltpu.HBM)],
        out_specs=(WHOLE, WHOLE),
        out_shape=(
            pltpu.VMEM((HALF, 6 * WIDTH), bf16),
            pltpu.VMEM((2, 3, SEQ, RUN, WIDTH), bf16),
        ),
        scratch_shapes=[pltpu.VMEM((2, HALF, ROWS), bf16), pltpu.SemaphoreType.DMA((2, 3))],
        compiler_params=pltpu.CompilerParams(vmem_limit_bytes=16 * MIB),
        name="unpack_first",
    )(flat, pltpu.with_memory_space_constraint(home, pltpu.HBM))


def unpack_last_kernel(flat_ref, rows_ref, own_ref):
    for h in range(2):
        gather(h, rows_ref, own_ref, places(1, h, flat_ref))


def unpack_last(flat, rows):
    return pl.pallas_call(
        unpack_last_kernel,
        in_specs=[WHOLE, WHOLE],
        out_specs=WHOLE,
        out_shape=pltpu.VMEM((HALF, 6 * WIDTH), bf16),
        compiler_params=pltpu.CompilerParams(vmem_limit_bytes=12 * MIB),
        name="unpack_last",
    )(flat, near(rows))


def merge_kernel(a_ref, b_ref, q_ref, k_ref, v_ref):
    i, j = iota((256, 256), 0), iota((256, 256), 1)
    merge = (i == jnp.where(j < 128, 2 * j, 2 * j - 255)).astype(f32).astype(bf16)
    for s, ref in enumerate((a_ref, b_ref)):
        for b in range(HALF // 128):
            rows = ref[128 * b : 128 * (b + 1), :]
            both = jnp.concatenate([rows[:, : 3 * WIDTH], rows[:, 3 * WIDTH :]], axis=0)
            mixed = dot(merge, both).astype(bf16)
            at = 2 * HALF * s + 256 * b
            q_ref[at : at + 256, :] = mixed[:, :WIDTH]
            k_ref[at : at + 256, :] = mixed[:, WIDTH : 2 * WIDTH]
            v_ref[at : at + 256, :] = mixed[:, 2 * WIDTH :]


def merge(own_a, own_b):
    one = jax.ShapeDtypeStruct((2 * TOK, WIDTH), bf16)
    return pl.pallas_call(
        merge_kernel,
        in_specs=[WHOLE, WHOLE],
        out_specs=(WHOLE,) * 3,
        out_shape=(one, one, one),
        compiler_params=pltpu.CompilerParams(vmem_limit_bytes=6 * MIB),
        cost_estimate=pl.CostEstimate(flops=10**9, bytes_accessed=3 * 10**6, transcendentals=0),
        name="merge",
    )(near(own_a), near(own_b))


def project_kernel(plan, count, skip, *refs):
    mine_ref, theirs_ref = refs[:2]
    outs = refs[-len(plan) :]
    grads, extra = refs[2 : 2 + count], refs[2 + count : -len(plan) - skip]
    for i, ((at, j), out) in enumerate(zip(plan, outs)):
        total = dot(grads[at][...], mine_ref[j]) + dot(grads[at + 1][...], theirs_ref[j])
        if extra and i == len(plan) - 1:
            total = total + extra[0][...].astype(f32)
        out[...] = total.astype(out.dtype)


def project(plan, types, mine, theirs, grads, extra=(), after=()):
    return pl.pallas_call(
        functools.partial(project_kernel, plan, len(grads), len(after)),
        in_specs=[WHOLE] * (2 + len(grads) + len(extra)) + [pl.BlockSpec(memory_space=pl.ANY)] * len(after),
        out_specs=(WHOLE,) * len(plan),
        out_shape=tuple(pltpu.VMEM((HALF, QUARTER), kind) for kind in types),
        compiler_params=pltpu.CompilerParams(vmem_limit_bytes=6 * MIB),
        cost_estimate=pl.CostEstimate(
            flops=len(plan) * 4 * HALF * QUARTER * 6 * WIDTH, bytes_accessed=10**6, transcendentals=0
        ),
        name="project",
    )(*[near(x) for x in (mine, theirs, *grads, *extra)], *after)


def finish_kernel(half, own_ref, got_ref, *refs):
    out_ref, turned_ref, sem = refs[-3:]
    turned_ref[...] = (own_ref[...] + got_ref[...].astype(f32)).T.astype(bf16)
    copy = pltpu.make_async_copy(turned_ref, out_ref.at[:, pl.ds(HALF * half, HALF)], sem)
    copy.start()
    copy.wait()


def finish(half, own, got, *whole):
    far = pl.BlockSpec(memory_space=pltpu.HBM)
    return pl.pallas_call(
        functools.partial(finish_kernel, half),
        in_specs=[WHOLE] * 2 + [far] * len(whole),
        out_specs=far,
        out_shape=jax.ShapeDtypeStruct((QUARTER, TOK), bf16),
        scratch_shapes=[pltpu.VMEM((QUARTER, HALF), bf16), pltpu.SemaphoreType.DMA],
        input_output_aliases={2: 0} if whole else {},
        compiler_params=pltpu.CompilerParams(vmem_limit_bytes=6 * MIB),
        name="finish",
    )(near(own), near(got), *whole)


def shards(queries, keys, values, out_grad, cluster_ids, query_weight, key_weight, value_weight):
    place = lax.axis_index("head")
    core, z = place % 2, place // 2
    swap = [(i, i ^ 1) for i in range(8)]
    up = [(i, (i + 2) % 8) for i in range(8)]
    down = [(i, (i - 2) % 8) for i in range(8)]

    def blocks(which):
        parts = [w.reshape(4, 2, QUARTER, 2, WIDTH) for w in (query_weight, key_weight, value_weight)]
        parts = [lax.dynamic_index_in_dim(w, which, 1, keepdims=False) for w in parts]
        whole = jnp.transpose(jnp.stack(parts, axis=3), (0, 2, 3, 4, 1)).reshape(4, 6 * WIDTH, QUARTER)
        return jnp.roll(whole, -z, axis=0)

    mine = blocks(core)
    theirs = lax.ppermute(blocks(1 - core), "head", swap)

    ids = jnp.transpose(cluster_ids, (0, 2, 1))
    flat2 = [x.reshape(2 * TOK, WIDTH) for x in (queries, keys, values, out_grad)]
    sent, flat = pack(ids, *flat2)
    got = lax.all_to_all(sent, "seq", split_axis=0, concat_axis=0, tiled=True)
    back, sums = attend(got)
    key_sums = jnp.transpose(sums, (1, 0, 2))
    home = lax.all_to_all(back, "seq", split_axis=0, concat_axis=0, tiled=True)
    flat, mine, theirs = lax.optimization_barrier((flat, mine, theirs))
    own_a, rows = unpack_first(flat, home)
    other_a = lax.ppermute(own_a, "head", swap)
    own_b = unpack_last(flat, rows)
    other_b = lax.ppermute(own_b, "head", swap)

    half_a, half_b = (own_a, other_a), (own_b, other_b)
    first, second = project(((0, 2), (0, 3)), (bf16, bf16), mine, theirs, half_a)
    far_a = lax.ppermute(first, "head", up)
    down_a = lax.ppermute(second, "head", down)
    far_b, up_b = project(((0, 2), (0, 1)), (bf16, bf16), mine, theirs, half_b, after=(first,))
    far_b = lax.ppermute(far_b, "head", down)
    up_b = lax.ppermute(up_b, "head", up)
    (last_b,) = project(((0, 3),), (f32,), mine, theirs, half_b)
    (sum_b,) = project(((0, 0),), (f32,), mine, theirs, half_b, (up_b,))
    down_b = lax.ppermute((last_b + far_b.astype(f32)).astype(bf16), "head", down)
    (next_a,) = project(((0, 1),), (f32,), mine, theirs, half_a)
    (sum_a,) = project(((0, 0),), (f32,), mine, theirs, half_a, (down_a,))
    up_a = lax.ppermute((next_a + far_a.astype(f32)).astype(bf16), "head", up)
    input_grad = finish(1, sum_b, down_b, finish(0, sum_a, up_a))
    grads = [x.reshape(TOK, 2, WIDTH) for x in merge(own_a, own_b)]
    return (*grads, input_grad, key_sums)


def solution(mesh):
    placed = (
        P("seq", "head", None),
        P("seq", "head", None),
        P("seq", "head", None),
        P("seq", "head", None),
        P("head", "seq", None),
        P(None, "head", None),
        P(None, "head", None),
        P(None, "head", None),
    )
    return jax.shard_map(
        shards,
        mesh=mesh,
        in_specs=placed,
        out_specs=(
            P("seq", "head", None),
            P("seq", "head", None),
            P("seq", "head", None),
            P("head", "seq"),
            P("head", "seq", None),
        ),
        check_vma=False,
    )
```
